32 devices in a mesh: groups: 2 (over y), wide: 4 (over z), narrow: 2 (over x), sub: 2 (over core).
Axes of the slice: x: 2, y: 2, z: 4, core: 2. Of those that a mesh axis runs over, the one named last changes fastest.
Arguments:
- amplitudes: bfloat16 [4, 2048, 7680], P(('narrow', 'sub'), 'groups', 'wide'), parts along dimension 1, may hold values from -6 to 6
- integrals: bfloat16 [4, 4, 48, 256, 256], P(('narrow', 'sub'), 'wide'), may hold values from -0.09375 to 0.09375
- tile_list: int32 [4, 4, 48, 2], P(('narrow', 'sub'), 'wide'), may hold values from 0 to 29, as said below
- tile_counts: int32 [4, 4], P(('narrow', 'sub'), 'wide'), may hold values from 12 to 48, as said below
Outputs:
- ladder: float32 [2048, 15360], P(('groups', 'narrow', 'sub'), 'wide'), parts along dimension 0
The draws below stay inside these ranges and needn't reach their ends.
There are 2 independent parts, one for each index of `groups`. The reference program is written for one: setup_inputs(seed, part) draws one part's arguments, and reference() takes and returns one part's arrays. A program takes and returns all parts, laid end to end along the dimension named above; an argument that names none is the same for every part. Nothing has to cross between parts.
Inputs may be any that keep to these rules, and one draw needn't show every extreme that they name: `tile_list`: slots of one device name distinct tiles; entry 0 is a row block below 30, entry 1 a column block below 15; slots at or past the device's count are not part of the sum. `tile_counts`: some device holds 48 live slots in every draw.
All inputs are finite; a program needn't handle non-finite values.
Results may differ from the reference program's by a relative error of at most 0.0003.
Values may be sent and summed in bfloat16 or wider, within the bound.
A program may use at most 128 MiB of HBM per device.

```python
import jax
import jax.numpy as jnp
from jax import lax

SLAB = 1024
PB = 256
RB_DEV = 30
CB_DEV = 15
TMAX = 48
NSDEV = 4
ROWS_DEV = 7680
NAB = 15360
N_WIDE = 4


def draw_tile_list(key, part):
    key = jax.random.fold_in(key, 5)
    subkeys = jax.random.split(key, NSDEV * N_WIDE)
    shuffled = jax.vmap(lambda one: jax.random.permutation(one, RB_DEV * CB_DEV)[:TMAX])(subkeys)
    rows_part = shuffled // CB_DEV
    cols_part = shuffled % CB_DEV
    joined = jnp.stack([rows_part, cols_part], axis=-1).astype(jnp.int32)
    return joined.reshape(NSDEV, N_WIDE, TMAX, 2)


def draw_tile_counts(key, part):
    key = jax.random.fold_in(key, 9)
    first_key, second_key = jax.random.split(key)
    counted = jax.random.randint(first_key, (NSDEV * N_WIDE,), max(1, TMAX // 4), TMAX + 1)
    fullest = jax.random.randint(second_key, (), 0, NSDEV * N_WIDE)
    counted = jnp.where(jnp.arange(NSDEV * N_WIDE) == fullest, TMAX, counted)
    return counted.astype(jnp.int32).reshape(NSDEV, N_WIDE)


def level_of(stream_key, dims, shards, least, top_value):
    gain, own = 1.0, jax.random.fold_in(stream_key, 6)
    for position, shards_of in shards:
        steps = jnp.exp(jax.random.uniform(jax.random.fold_in(own, position), (shards_of,), jnp.float32, least / len(shards), top_value / len(shards)))
        gain = gain * jnp.repeat(steps, dims[position] // shards_of).reshape([-1 if axis == position else 1 for axis in range(len(dims))])
    return gain


def bell_draw(stream_key, shape, width, reach, shards=(), kind=jnp.bfloat16):
    drawn = jax.random.normal(stream_key, shape, jnp.float32) * width
    if len(shards) > 0:
        drawn = level_of(stream_key, shape, shards, -0.22, 0.18) * drawn
    return jnp.clip(drawn, min=-reach, max=reach).astype(kind)


def setup_inputs(seed: int = 0, part: int = 0) -> dict:
    streams_of = jax.random.split(jax.random.key(seed), 5)
    own_keys = jax.random.split(jax.random.fold_in(streams_of[4], part), 5)
    return {
        "amplitudes": bell_draw(own_keys[0], (NSDEV, SLAB, ROWS_DEV), 1.0, 6.0, ((0, 4), (2, 4))),
        "integrals": bell_draw(streams_of[1], (NSDEV, N_WIDE, TMAX, PB, PB), (16 * PB) ** -0.5, 0.09375, ((0, 4), (1, 4))),
        "tile_list": draw_tile_list(jax.random.fold_in(streams_of[4], 71), part),
        "tile_counts": draw_tile_counts(jax.random.fold_in(streams_of[4], 71), part),
    }


def region(amp_rows, tile_block, listed, live_count):
    blocks = amp_rows.reshape(SLAB, RB_DEV, PB)
    chosen = jnp.take(blocks, listed[:, 0].astype(jnp.int32), axis=1)
    products = jnp.einsum("stp,tpq->tsq", chosen.astype(jnp.float32), tile_block.astype(jnp.float32), precision=lax.Precision.HIGHEST)
    live = (jnp.arange(TMAX) < live_count).astype(jnp.float32)
    onehot = (listed[:, 1][None, :] == jnp.arange(CB_DEV)[:, None]).astype(jnp.float32) * live[None, :]
    partial_value = jnp.einsum("ct,tsq->scq", onehot, products, precision=lax.Precision.HIGHEST)
    return partial_value.reshape(SLAB, CB_DEV * PB)


def reference(amplitudes, integrals, tile_list, tile_counts):
    def column(column_index):
        def step(total, row_index):
            term = region(amplitudes[row_index], integrals[row_index, column_index], tile_list[row_index, column_index], tile_counts[row_index, column_index])
            return total + term, None
        start = jnp.zeros((SLAB, CB_DEV * PB), jnp.float32)
        total, unused = lax.scan(step, start, jnp.arange(NSDEV))
        return total
    columns = lax.map(column, jnp.arange(N_WIDE))
    return jnp.transpose(columns, (1, 0, 2)).reshape(SLAB, NAB)
```

```python
import functools

import jax
import jax.numpy as jnp
from jax import lax
from jax.experimental import pallas as pl
from jax.experimental.pallas import tpu as pltpu
from jax.sharding import PartitionSpec as P

CB_DEV = 15
CHUNKS = 8
MESH = pl.DeviceIdType.MESH


def group_width(slot_count):
    best = 1
    for candidate in range(1, 9):
        if slot_count % candidate == 0:
            best = candidate
    return best


def gathered_shards(amplitudes, integrals, tile_list, tile_counts):
    gathered = lax.all_gather(amplitudes[0], "wide", axis=1, tiled=True)
    tile_block = integrals[0, 0]
    listed = tile_list[0, 0]
    live_count = tile_counts[0, 0]
    slab_rows = gathered.shape[0]
    block_size = tile_block.shape[1]
    slot_count = tile_block.shape[0]
    row_blocks = gathered.shape[1] // block_size
    blocks = gathered.reshape(slab_rows, row_blocks, block_size)
    width = group_width(slot_count)
    group_total = (live_count + width - 1) // width

    def add_group(group_index, total):
        first = group_index * width
        these = lax.dynamic_slice_in_dim(listed, first, width, 0)
        tiles_here = lax.dynamic_slice_in_dim(tile_block, first, width, 0)
        chosen = jnp.take(blocks, these[:, 0], axis=1)
        products = jnp.einsum(
            "stp,tpq->tsq", chosen, tiles_here, preferred_element_type=jnp.float32
        )
        live = (first + jnp.arange(width) < live_count).astype(jnp.float32)
        for member in range(width):
            column_start = these[member, 1] * block_size
            current = lax.dynamic_slice_in_dim(total, column_start, block_size, 1)
            updated = current + products[member] * live[member]
            total = lax.dynamic_update_slice_in_dim(total, updated, column_start, 1)
        return total

    empty = jnp.zeros((slab_rows, CB_DEV * block_size), jnp.float32)
    partial_value = lax.fori_loop(0, group_total, add_group, empty)
    result = lax.psum_scatter(partial_value, ("narrow", "sub"), scatter_dimension=0, tiled=True)
    return result


def tile_order(listed, live_count):
    count = listed.shape[0]
    place = jnp.arange(count, dtype=jnp.int32)
    column = jnp.where(place < live_count, listed[:, 1], CB_DEV)
    key = column * count + place
    rank = jnp.sum((key[None, :] < key[:, None]).astype(jnp.int32), axis=1)
    at = (rank[None, :] == place[:, None]).astype(jnp.int32)
    order = jnp.sum(at * place[None, :], axis=1)
    rows = jnp.sum(at * listed[None, :, 0], axis=1)
    first = jnp.sum((column[None, :] < column[:, None]).astype(jnp.int32), axis=1)
    keep = jnp.sum(at * (first != rank).astype(jnp.int32)[None, :], axis=1)
    columns = jnp.arange(CB_DEV, dtype=jnp.int32)
    here = jnp.sum((column[None, :] == columns[:, None]).astype(jnp.int32), axis=1)
    upto = jnp.sum((column[None, :] <= columns[:, None]).astype(jnp.int32), axis=1)
    last = jnp.where(here > 0, upto - 1, count)
    return order, rows, keep, last


def ladder_kernel(
    n_wide,
    order, rows_of, keep, last, amp, tiles, out,
    held, mine, tile_held, sums, first_out, first_in, total, second_out, second_in,
    own_sem, tile_sem, left_sem, right_sem, come_sem,
    first_send, first_recv, second_send, second_recv, out_sem,
):
    w = lax.axis_index("wide")
    n = lax.axis_index("narrow")
    s = lax.axis_index("sub")
    quarters, quarter_rows, piece = amp.shape
    step = quarter_rows // CHUNKS
    slots, block, _ = tiles.shape
    strips = n_wide * piece // 128
    per_block = block // 128

    barrier = pltpu.get_barrier_semaphore()
    pl.semaphore_signal(barrier, inc=1, device_id={"sub": 1 - s}, device_id_type=MESH)
    pl.semaphore_signal(barrier, inc=1, device_id={"narrow": 1 - n}, device_id_type=MESH)

    @pl.when(w > 0)
    def _():
        pl.semaphore_signal(barrier, inc=1, device_id={"wide": w - 1}, device_id_type=MESH)

    @pl.when(w < n_wide - 1)
    def _():
        pl.semaphore_signal(barrier, inc=1, device_id={"wide": w + 1}, device_id_type=MESH)

    own_copy = pltpu.make_async_copy(
        amp, held.at[:, :, pl.ds(pl.multiple_of(w * piece, 128), piece)], own_sem
    )
    own_copy.start()
    tile_copy = pltpu.make_async_copy(tiles, tile_held, tile_sem)
    tile_copy.start()
    sums[slots] = jnp.zeros(sums.shape[1:], jnp.float32)

    at_end = (w == 0) | (w == n_wide - 1)
    pl.semaphore_wait(barrier, jnp.where(at_end, 3, 4) if n_wide > 1 else 2)

    def some(c):
        return pl.ds(pl.multiple_of(c * step, step), step)

    def part(origin, c):
        return held.at[:, some(c), pl.ds(pl.multiple_of(origin * piece, 128), piece)]

    def to_left(origin, c, source=None):
        return pltpu.make_async_remote_copy(
            src_ref=part(origin, c) if source is None else source,
            dst_ref=part(origin, c),
            send_sem=left_sem.at[origin, c],
            recv_sem=come_sem.at[origin, c],
            device_id={"wide": w - 1},
            device_id_type=MESH,
        )

    def to_right(origin, c, source=None):
        return pltpu.make_async_remote_copy(
            src_ref=part(origin, c) if source is None else source,
            dst_ref=part(origin, c),
            send_sem=right_sem.at[origin, c],
            recv_sem=come_sem.at[origin, c],
            device_id={"wide": w + 1},
            device_id_type=MESH,
        )

    def send_own(c):
        @pl.when(w > 0)
        def _():
            to_left(w, c, amp.at[:, some(c), :]).start()

        @pl.when(w < n_wide - 1)
        def _():
            to_right(w, c, amp.at[:, some(c), :]).start()

    def first_copy(c):
        return pltpu.make_async_remote_copy(
            src_ref=first_out.at[c],
            dst_ref=first_in.at[c],
            send_sem=first_send.at[c],
            recv_sem=first_recv.at[c],
            device_id={"sub": 1 - s},
            device_id_type=MESH,
        )

    def second_copy(c):
        return pltpu.make_async_remote_copy(
            src_ref=second_out.at[c],
            dst_ref=second_in.at[c],
            send_sem=second_send.at[c],
            recv_sem=second_recv.at[c],
            device_id={"narrow": 1 - n},
            device_id_type=MESH,
        )

    def out_copy(c):
        return pltpu.make_async_copy(second_in.at[c], out.at[some(c), :], out_sem.at[c])

    send_own(0)
    send_own(1)
    own_copy.wait()
    tile_copy.wait()

    def turn(c, nothing):
        @pl.when(c < CHUNKS)
        def _():
            @pl.when(c + 2 < CHUNKS)
            def _():
                send_own(c + 2)

            for distance in range(1, n_wide):
                @pl.when(w + distance < n_wide)
                def _():
                    to_left(w + distance, c).wait_recv()

                    @pl.when(w > 0)
                    def _():
                        to_left(w + distance, c).start()

                @pl.when(w - distance >= 0)
                def _():
                    to_right(w - distance, c).wait_recv()

                    @pl.when(w < n_wide - 1)
                    def _():
                        to_right(w - distance, c).start()

            for half in range(2):
                for place, quarter in ((half, 2 * half + 1 - s), (2 + half, 2 * half + s)):
                    for strip in range(strips):
                        mine[strip, place] = held[quarter, some(c), pl.ds(strip * 128, 128)]

            def multiply(t, so_far):
                chosen = jnp.concatenate(
                    [
                        mine[rows_of[t] * per_block + strip].reshape(quarters * step, 128)
                        for strip in range(per_block)
                    ],
                    axis=1,
                )
                product = jnp.dot(
                    chosen, tile_held[order[t]], preferred_element_type=jnp.float32
                )
                so_far = so_far * keep[t].astype(jnp.float32) + product
                sums[t] = so_far.reshape(quarters, step, block)
                return so_far

            lax.fori_loop(
                0, slots, multiply, jnp.zeros((quarters * step, block), jnp.float32)
            )

            slot = lax.rem(c, 3)
            for b in range(CB_DEV):
                columns = pl.ds(b * block, block)
                column_sum = sums[last[b]]
                first_out[c, :, :, columns] = column_sum[:2]
                total[slot, :, :, columns] = column_sum[2:]
            first_copy(c).start()

        @pl.when((c >= 1) & (c <= CHUNKS))
        def _():
            e = c - 1
            slot = lax.rem(e, 3)
            first_copy(e).wait_recv()
            second_out[e] = total[slot, 1 - n] + first_in[e, 1 - n]
            second_copy(e).start()
            total[slot, n] = total[slot, n] + first_in[e, n]

        @pl.when(c >= 2)
        def _():
            e = c - 2
            second_copy(e).wait_recv()
            second_in[e] = second_in[e] + total[lax.rem(e, 3), n]
            out_copy(e).start()

        return nothing

    lax.fori_loop(0, CHUNKS + 2, turn, 0)

    def finish(c, nothing):
        for origin in range(n_wide):
            @pl.when((w > 0) & (origin >= w))
            def _():
                to_left(origin, c).wait_send()

            @pl.when((w < n_wide - 1) & (origin <= w))
            def _():
                to_right(origin, c).wait_send()

        first_copy(c).wait_send()
        second_copy(c).wait_send()
        out_copy(c).wait()
        return nothing

    lax.fori_loop(0, CHUNKS, finish, 0)


def fused_shards(n_wide, amplitudes, integrals, tile_list, tile_counts):
    _, slab_rows, piece = amplitudes.shape
    slots, block = integrals.shape[2], integrals.shape[3]
    quarter_rows = slab_rows // 4
    step = quarter_rows // CHUNKS
    width = CB_DEV * block
    ordered = tile_order(tile_list[0, 0], tile_counts[0, 0])
    in_smem = pl.BlockSpec(memory_space=pltpu.SMEM)
    anywhere = pl.BlockSpec(memory_space=pl.ANY)
    dma = pltpu.SemaphoreType.DMA
    return pl.pallas_call(
        functools.partial(ladder_kernel, n_wide),
        out_shape=jax.ShapeDtypeStruct((quarter_rows, width), jnp.float32),
        in_specs=[in_smem] * 4 + [anywhere] * 2,
        out_specs=anywhere,
        scratch_shapes=[
            pltpu.VMEM((4, quarter_rows, n_wide * piece), jnp.bfloat16),
            pltpu.VMEM((n_wide * piece // 128, 4, step, 128), jnp.bfloat16),
            pltpu.VMEM((slots, block, block), jnp.bfloat16),
            pltpu.VMEM((slots + 1, 4, step, block), jnp.float32),
            pltpu.VMEM((CHUNKS, 2, step, width), jnp.float32),
            pltpu.VMEM((CHUNKS, 2, step, width), jnp.float32),
            pltpu.VMEM((3, 2, step, width), jnp.float32),
            pltpu.VMEM((CHUNKS, step, width), jnp.float32),
            pltpu.VMEM((CHUNKS, step, width), jnp.float32),
            dma, dma,
            dma((n_wide, CHUNKS)), dma((n_wide, CHUNKS)), dma((n_wide, CHUNKS)),
            dma((CHUNKS,)), dma((CHUNKS,)), dma((CHUNKS,)), dma((CHUNKS,)), dma((CHUNKS,)),
        ],
        compiler_params=pltpu.CompilerParams(
            collective_id=0, has_side_effects=True, vmem_limit_bytes=63 * 1024 * 1024
        ),
    )(*ordered, amplitudes.reshape(4, quarter_rows, piece), integrals[0, 0])


def shards(sizes, amplitudes, integrals, tile_list, tile_counts):
    fits = (
        sizes["narrow"] == 2
        and sizes["sub"] == 2
        and sizes["wide"] <= 4
        and amplitudes.shape[2] % 128 == 0
    )
    if fits:
        return fused_shards(sizes["wide"], amplitudes, integrals, tile_list, tile_counts)
    return gathered_shards(amplitudes, integrals, tile_list, tile_counts)


def solution(mesh):
    placed = (
        P(("narrow", "sub"), "groups", "wide"),
        P(("narrow", "sub"), "wide", None, None, None),
        P(("narrow", "sub"), "wide", None, None),
        P(("narrow", "sub"), "wide"),
    )
    return jax.shard_map(
        functools.partial(shards, dict(mesh.shape)),
        mesh=mesh,
        in_specs=placed,
        out_specs=P(("groups", "narrow", "sub"), "wide"),
        check_vma=False,
    )
```

```python
import functools

import jax
import jax.numpy as jnp
from jax import lax
from jax.experimental import pallas as pl
from jax.experimental.pallas import tpu as pltpu
from jax.sharding import PartitionSpec as P

CB_DEV = 15
CHUNKS = 8
HOME = 4
UNITS = HOME + 2 * (CHUNKS - HOME)
TILE_PARTS = 4
MESH = pl.DeviceIdType.MESH


def group_width(slot_count):
    best = 1
    for candidate in range(1, 9):
        if slot_count % candidate == 0:
            best = candidate
    return best


def gathered_shards(amplitudes, integrals, tile_list, tile_counts):
    gathered = lax.all_gather(amplitudes[0], "wide", axis=1, tiled=True)
    tile_block = integrals[0, 0]
    listed = tile_list[0, 0]
    live_count = tile_counts[0, 0]
    slab_rows = gathered.shape[0]
    block_size = tile_block.shape[1]
    slot_count = tile_block.shape[0]
    row_blocks = gathered.shape[1] // block_size
    blocks = gathered.reshape(slab_rows, row_blocks, block_size)
    width = group_width(slot_count)
    group_total = (live_count + width - 1) // width

    def add_group(group_index, total):
        first = group_index * width
        these = lax.dynamic_slice_in_dim(listed, first, width, 0)
        tiles_here = lax.dynamic_slice_in_dim(tile_block, first, width, 0)
        chosen = jnp.take(blocks, these[:, 0], axis=1)
        products = jnp.einsum(
            "stp,tpq->tsq", chosen, tiles_here, preferred_element_type=jnp.float32
        )
        live = (first + jnp.arange(width) < live_count).astype(jnp.float32)
        for member in range(width):
            column_start = these[member, 1] * block_size
            current = lax.dynamic_slice_in_dim(total, column_start, block_size, 1)
            updated = current + products[member] * live[member]
            total = lax.dynamic_update_slice_in_dim(total, updated, column_start, 1)
        return total

    empty = jnp.zeros((slab_rows, CB_DEV * block_size), jnp.float32)
    partial_value = lax.fori_loop(0, group_total, add_group, empty)
    result = lax.psum_scatter(partial_value, ("narrow", "sub"), scatter_dimension=0, tiled=True)
    return result


def tile_order(listed, live_count):
    count = listed.shape[0]
    place = jnp.arange(count, dtype=jnp.int32)
    column = jnp.where(place < live_count, listed[:, 1], CB_DEV)
    key = column * count + place
    rank = jnp.sum((key[None, :] < key[:, None]).astype(jnp.int32), axis=1)
    at = (rank[None, :] == place[:, None]).astype(jnp.int32)
    order = jnp.sum(at * place[None, :], axis=1)
    rows = jnp.sum(at * listed[None, :, 0], axis=1)
    first = jnp.sum((column[None, :] < column[:, None]).astype(jnp.int32), axis=1)
    keep = jnp.sum(at * (first != rank).astype(jnp.int32)[None, :], axis=1)
    columns = jnp.arange(CB_DEV, dtype=jnp.int32)
    here = jnp.sum((column[None, :] == columns[:, None]).astype(jnp.int32), axis=1)
    upto = jnp.sum((column[None, :] <= columns[:, None]).astype(jnp.int32), axis=1)
    last = jnp.where(here > 0, upto - 1, count)
    lines = [jnp.pad(line, (0, 128 - line.shape[0])) for line in (order, rows, keep, last)]
    return jnp.pad(jnp.stack(lines), ((0, 4), (0, 0)))


def ladder_kernel(
    n_wide,
    own_list, amp, tiles, list_source, out, list_landed,
    held, mine, own_tiles, end_tiles, end_list, sums,
    first_out, first_in, total, second_out, second_in,
    own_sem, tile_sem, list_sem, left_sem, right_sem, come_sem,
    first_send, first_recv, second_send, second_recv, out_sem,
    part_send, part_recv, across_send, across_recv,
    list_send, list_recv, back_send, back_recv,
):
    g = lax.axis_index("groups")
    w = lax.axis_index("wide")
    n = lax.axis_index("narrow")
    s = lax.axis_index("sub")
    quarters, quarter_rows, piece = amp.shape
    step = quarter_rows // CHUNKS
    slots, block, _ = tiles.shape
    strips = n_wide * piece // 128
    per_block = block // 128
    is_end = (w == 0) | (w == n_wide - 1)
    is_inner = (w > 0) & (w < n_wide - 1)
    mate = w + 1 - 2 * lax.rem(w, 2)
    part_slots = slots // 2 // TILE_PARTS

    barrier = pltpu.get_barrier_semaphore()
    pl.semaphore_signal(barrier, inc=1, device_id={"sub": 1 - s}, device_id_type=MESH)
    pl.semaphore_signal(barrier, inc=1, device_id={"narrow": 1 - n}, device_id_type=MESH)

    @pl.when(is_inner)
    def _():
        pl.semaphore_signal(barrier, inc=1, device_id={"groups": 1 - g}, device_id_type=MESH)

    @pl.when(w > 0)
    def _():
        pl.semaphore_signal(barrier, inc=1, device_id={"wide": w - 1}, device_id_type=MESH)

    @pl.when(w < n_wide - 1)
    def _():
        pl.semaphore_signal(barrier, inc=1, device_id={"wide": w + 1}, device_id_type=MESH)

    own_copy = pltpu.make_async_copy(
        amp, held.at[:, :, pl.ds(pl.multiple_of(w * piece, 128), piece)], own_sem
    )
    own_copy.start()
    tile_copy = pltpu.make_async_copy(tiles, own_tiles, tile_sem)
    tile_copy.start()
    sums[slots] = jnp.zeros(sums.shape[1:], jnp.float32)

    pl.semaphore_wait(barrier, jnp.where(is_end, 3, 5))

    def some(c):
        return pl.ds(pl.multiple_of(c * step, step), step)

    def part(origin, c):
        return held.at[:, some(c), pl.ds(pl.multiple_of(origin * piece, 128), piece)]

    def remote(source, target, send, recv, device):
        return pltpu.make_async_remote_copy(
            src_ref=source, dst_ref=target, send_sem=send, recv_sem=recv,
            device_id=device, device_id_type=MESH,
        )

    def to_left(origin, c, source=None):
        return remote(
            part(origin, c) if source is None else source, part(origin, c),
            left_sem.at[origin, c], come_sem.at[origin, c], {"wide": w - 1},
        )

    def to_right(origin, c, source=None):
        return remote(
            part(origin, c) if source is None else source, part(origin, c),
            right_sem.at[origin, c], come_sem.at[origin, c], {"wide": w + 1},
        )

    def left_takes(c):
        return (w > 1) | ((w == 1) & (c < HOME))

    def right_takes(c):
        return (w < n_wide - 2) | ((w == n_wide - 2) & (c < HOME))

    def send_own(c):
        @pl.when(left_takes(c))
        def _():
            to_left(w, c, amp.at[:, some(c), :]).start()

        @pl.when(right_takes(c))
        def _():
            to_right(w, c, amp.at[:, some(c), :]).start()

    def part_copy(p):
        here = pl.ds(g * (slots // 2) + p * part_slots, part_slots)
        return remote(
            tiles.at[here], end_tiles.at[here], part_send.at[p], part_recv.at[p], {"wide": mate}
        )

    def across_copy(p):
        here = pl.ds(g * (slots // 2) + p * part_slots, part_slots)
        return remote(
            end_tiles.at[here], end_tiles.at[here],
            across_send.at[p], across_recv.at[p], {"groups": 1 - g},
        )

    list_copy = remote(list_source, list_landed, list_send, list_recv, {"wide": mate})

    def first_copy(u):
        return remote(
            first_out.at[lax.rem(u, 2)], first_in.at[u],
            first_send.at[u], first_recv.at[u], {"sub": 1 - s},
        )

    def second_copy(u):
        return remote(
            second_out.at[lax.rem(u, 2)], second_in.at[u],
            second_send.at[u], second_recv.at[u], {"narrow": 1 - n},
        )

    def out_copy(u, c):
        return pltpu.make_async_copy(second_in.at[u], out.at[some(c), :], out_sem.at[c])

    def back_copy(u, c):
        return remote(
            second_in.at[u], out.at[some(c), :], back_send.at[c], back_recv.at[c], {"wide": mate}
        )

    def chunk_of(u):
        return jnp.where(u < HOME, u, lax.div(u, 2) + HOME // 2)

    def active(u):
        return (u >= 0) & ((u < HOME) | (is_inner & (u < UNITS)))

    def for_mate(u):
        return (u >= HOME) & (lax.rem(u, 2) == 0)

    def compute(u, tile_ref, listed):
        def multiply(t, so_far):
            chosen = jnp.concatenate(
                [
                    mine[listed[1, t] * per_block + strip].reshape(quarters * step, 128)
                    for strip in range(per_block)
                ],
                axis=1,
            )
            product = jnp.dot(
                chosen, tile_ref[listed[0, t]], preferred_element_type=jnp.float32
            )
            so_far = so_far * listed[2, t].astype(jnp.float32) + product
            sums[t] = so_far.reshape(quarters, step, block)
            return so_far

        lax.fori_loop(0, slots, multiply, jnp.zeros((quarters * step, block), jnp.float32))
        slot, side = lax.rem(u, 3), lax.rem(u, 2)
        for b in range(CB_DEV):
            columns = pl.ds(b * block, block)
            column_sum = sums[listed[3, b]]
            first_out[side, :, :, columns] = column_sum[:2]
            total[slot, :, :, columns] = column_sum[2:]
        first_copy(u).start()

    send_own(0)

    @pl.when(is_end)
    def _():
        list_copy.start()
        part_copy(0).start()

    send_own(1)
    own_copy.wait()
    tile_copy.wait()

    def turn(u, nothing):
        c = chunk_of(u)
        opens = (u < HOME) | (lax.rem(u, 2) == 0)

        @pl.when(opens & (c + 2 < CHUNKS))
        def _():
            send_own(c + 2)

        @pl.when(is_end & (u + 1 < TILE_PARTS))
        def _():
            part_copy(u + 1).start()

        @pl.when(is_inner & (u >= 1) & (u <= TILE_PARTS))
        def _():
            part_copy(u - 1).wait_recv()
            across_copy(u - 1).start()

        @pl.when(active(u) & opens)
        def _():
            for distance in range(1, n_wide):
                @pl.when(w + distance < n_wide)
                def _():
                    to_left(w + distance, c).wait_recv()

                    @pl.when(left_takes(c))
                    def _():
                        to_left(w + distance, c).start()

                @pl.when(w - distance >= 0)
                def _():
                    to_right(w - distance, c).wait_recv()

                    @pl.when(right_takes(c))
                    def _():
                        to_right(w - distance, c).start()

            for half in range(2):
                for place, quarter in ((half, 2 * half + 1 - s), (2 + half, 2 * half + s)):
                    for strip in range(strips):
                        mine[strip, place] = held[quarter, some(c), pl.ds(strip * 128, 128)]

        @pl.when(is_inner & (u == TILE_PARTS))
        def _():
            list_copy.wait_recv()
            to_list = pltpu.make_async_copy(list_landed, end_list, list_sem)
            to_list.start()
            to_list.wait()
            for p in range(TILE_PARTS):
                across_copy(p).wait_recv()

        @pl.when(active(u) & jnp.logical_not(for_mate(u)))
        def _():
            compute(u, own_tiles, own_list)

        @pl.when(active(u) & for_mate(u))
        def _():
            compute(u, end_tiles, end_list)

        e = u - 1

        @pl.when(active(e))
        def _():
            slot = lax.rem(e, 3)
            first_copy(e).wait()
            second_out[lax.rem(e, 2)] = total[slot, 1 - n] + first_in[e, 1 - n]
            second_copy(e).start()
            total[slot, n] = total[slot, n] + first_in[e, n]

        f = u - 2

        @pl.when(active(f))
        def _():
            second_copy(f).wait()
            second_in[f] = second_in[f] + total[lax.rem(f, 3), n]

            @pl.when(for_mate(f))
            def _():
                back_copy(f, chunk_of(f)).start()

            @pl.when(jnp.logical_not(for_mate(f)))
            def _():
                out_copy(f, chunk_of(f)).start()

        return nothing

    lax.fori_loop(0, UNITS + 2, turn, 0)

    def finish(c, nothing):
        for origin in range(n_wide):
            @pl.when(left_takes(c) & (origin >= w))
            def _():
                to_left(origin, c).wait_send()

            @pl.when(right_takes(c) & (origin <= w))
            def _():
                to_right(origin, c).wait_send()

        @pl.when(is_inner | (c < HOME))
        def _():
            out_copy(0, c).wait()

        @pl.when(is_inner & (c >= HOME))
        def _():
            back_copy(0, c).wait_send()

        @pl.when(is_end & (c >= HOME))
        def _():
            back_copy(0, c).wait_recv()

        return nothing

    lax.fori_loop(0, CHUNKS, finish, 0)

    @pl.when(is_end)
    def _():
        list_copy.wait_send()
        for p in range(TILE_PARTS):
            part_copy(p).wait_send()

    @pl.when(is_inner)
    def _():
        for p in range(TILE_PARTS):
            across_copy(p).wait_send()


def fused_shards(n_wide, amplitudes, integrals, tile_list, tile_counts):
    _, slab_rows, piece = amplitudes.shape
    slots, block = integrals.shape[2], integrals.shape[3]
    quarter_rows = slab_rows // 4
    step = quarter_rows // CHUNKS
    width = CB_DEV * block
    listed = tile_order(tile_list[0, 0], tile_counts[0, 0])
    anywhere = pl.BlockSpec(memory_space=pl.ANY)
    dma = pltpu.SemaphoreType.DMA
    result, _ = pl.pallas_call(
        functools.partial(ladder_kernel, n_wide),
        out_shape=(
            jax.ShapeDtypeStruct((quarter_rows, width), jnp.float32),
            jax.ShapeDtypeStruct(listed.shape, jnp.int32),
        ),
        in_specs=[pl.BlockSpec(memory_space=pltpu.SMEM)] + [anywhere] * 3,
        out_specs=(anywhere, anywhere),
        scratch_shapes=[
            pltpu.VMEM((4, quarter_rows, n_wide * piece), jnp.bfloat16),
            pltpu.VMEM((n_wide * piece // 128, 4, step, 128), jnp.bfloat16),
            pltpu.VMEM((slots, block, block), jnp.bfloat16),
            pltpu.VMEM((slots, block, block), jnp.bfloat16),
            pltpu.SMEM(listed.shape, jnp.int32),
            pltpu.VMEM((slots + 1, 4, step, block), jnp.float32),
            pltpu.VMEM((2, 2, step, width), jnp.float32),
            pltpu.VMEM((UNITS, 2, step, width), jnp.float32),
            pltpu.VMEM((3, 2, step, width), jnp.float32),
            pltpu.VMEM((2, step, width), jnp.float32),
            pltpu.VMEM((UNITS, step, width), jnp.float32),
            dma, dma, dma,
            dma((n_wide, CHUNKS)), dma((n_wide, CHUNKS)), dma((n_wide, CHUNKS)),
            dma((UNITS,)), dma((UNITS,)), dma((UNITS,)), dma((UNITS,)), dma((CHUNKS,)),
            dma((TILE_PARTS,)), dma((TILE_PARTS,)), dma((TILE_PARTS,)), dma((TILE_PARTS,)),
            dma, dma, dma((CHUNKS,)), dma((CHUNKS,)),
        ],
        compiler_params=pltpu.CompilerParams(
            collective_id=0, has_side_effects=True, vmem_limit_bytes=63 * 1024 * 1024
        ),
    )(listed, amplitudes.reshape(4, quarter_rows, piece), integrals[0, 0], listed)
    return result


def shards(sizes, amplitudes, integrals, tile_list, tile_counts):
    fits = (
        sizes["narrow"] == 2
        and sizes["sub"] == 2
        and sizes["wide"] == 4
        and sizes["groups"] == 2
        and amplitudes.shape[2] % 128 == 0
    )
    if fits:
        return fused_shards(sizes["wide"], amplitudes, integrals, tile_list, tile_counts)
    return gathered_shards(amplitudes, integrals, tile_list, tile_counts)


def solution(mesh):
    placed = (
        P(("narrow", "sub"), "groups", "wide"),
        P(("narrow", "sub"), "wide", None, None, None),
        P(("narrow", "sub"), "wide", None, None),
        P(("narrow", "sub"), "wide"),
    )
    return jax.shard_map(
        functools.partial(shards, dict(mesh.shape)),
        mesh=mesh,
        in_specs=placed,
        out_specs=P(("groups", "narrow", "sub"), "wide"),
        check_vma=False,
    )
```

```python
import functools

import jax
import jax.numpy as jnp
from jax import lax
from jax.experimental import pallas as pl
from jax.experimental.pallas import tpu as pltpu
from jax.sharding import PartitionSpec as P

CB_DEV = 15
CHUNKS = 8
HOME = 6
LEAD = 4
UNITS = HOME + 2 * (CHUNKS - HOME)
TILE_PARTS = 4
MESH = pl.DeviceIdType.MESH


def group_width(slot_count):
    best = 1
    for candidate in range(1, 9):
        if slot_count % candidate == 0:
            best = candidate
    return best


def gathered_shards(amplitudes, integrals, tile_list, tile_counts):
    gathered = lax.all_gather(amplitudes[0], "wide", axis=1, tiled=True)
    tile_block = integrals[0, 0]
    listed = tile_list[0, 0]
    live_count = tile_counts[0, 0]
    slab_rows = gathered.shape[0]
    block_size = tile_block.shape[1]
    slot_count = tile_block.shape[0]
    row_blocks = gathered.shape[1] // block_size
    blocks = gathered.reshape(slab_rows, row_blocks, block_size)
    width = group_width(slot_count)
    group_total = (live_count + width - 1) // width

    def add_group(group_index, total):
        first = group_index * width
        these = lax.dynamic_slice_in_dim(listed, first, width, 0)
        tiles_here = lax.dynamic_slice_in_dim(tile_block, first, width, 0)
        chosen = jnp.take(blocks, these[:, 0], axis=1)
        products = jnp.einsum(
            "stp,tpq->tsq", chosen, tiles_here, preferred_element_type=jnp.float32
        )
        live = (first + jnp.arange(width) < live_count).astype(jnp.float32)
        for member in range(width):
            column_start = these[member, 1] * block_size
            current = lax.dynamic_slice_in_dim(total, column_start, block_size, 1)
            updated = current + products[member] * live[member]
            total = lax.dynamic_update_slice_in_dim(total, updated, column_start, 1)
        return total

    empty = jnp.zeros((slab_rows, CB_DEV * block_size), jnp.float32)
    partial_value = lax.fori_loop(0, group_total, add_group, empty)
    result = lax.psum_scatter(partial_value, ("narrow", "sub"), scatter_dimension=0, tiled=True)
    return result


def tile_order(listed, live_count):
    count = listed.shape[0]
    place = jnp.arange(count, dtype=jnp.int32)
    column = jnp.where(place < live_count, listed[:, 1], CB_DEV)
    key = column * count + place
    rank = jnp.sum((key[None, :] < key[:, None]).astype(jnp.int32), axis=1)
    at = (rank[None, :] == place[:, None]).astype(jnp.int32)
    order = jnp.sum(at * place[None, :], axis=1)
    rows = jnp.sum(at * listed[None, :, 0], axis=1)
    first = jnp.sum((column[None, :] < column[:, None]).astype(jnp.int32), axis=1)
    keep = jnp.sum(at * (first != rank).astype(jnp.int32)[None, :], axis=1)
    columns = jnp.arange(CB_DEV, dtype=jnp.int32)
    here = jnp.sum((column[None, :] == columns[:, None]).astype(jnp.int32), axis=1)
    upto = jnp.sum((column[None, :] <= columns[:, None]).astype(jnp.int32), axis=1)
    last = jnp.where(here > 0, upto - 1, count)
    lines = [jnp.pad(line, (0, 128 - line.shape[0])) for line in (order, rows, keep, last)]
    return jnp.pad(jnp.stack(lines), ((0, 4), (0, 0)))


def ladder_kernel(
    n_wide,
    own_list, amp, tiles, list_source, out, list_landed,
    held, mine, own_tiles, end_tiles, end_list, sums,
    first_out, first_in, total, second_out, second_in,
    own_sem, tile_sem, list_sem, left_sem, right_sem, come_sem,
    first_send, first_recv, second_send, second_recv, out_sem,
    part_send, part_recv, across_send, across_recv,
    list_send, list_recv, back_send, back_recv,
):
    g = lax.axis_index("groups")
    w = lax.axis_index("wide")
    n = lax.axis_index("narrow")
    s = lax.axis_index("sub")
    quarters, quarter_rows, piece = amp.shape
    step = quarter_rows // CHUNKS
    slots, block, _ = tiles.shape
    strips = n_wide * piece // 128
    per_block = block // 128
    is_end = (w == 0) | (w == n_wide - 1)
    is_inner = (w > 0) & (w < n_wide - 1)
    mate = w + 1 - 2 * lax.rem(w, 2)
    part_slots = slots // 2 // TILE_PARTS

    barrier = pltpu.get_barrier_semaphore()
    pl.semaphore_signal(barrier, inc=1, device_id={"sub": 1 - s}, device_id_type=MESH)
    pl.semaphore_signal(barrier, inc=1, device_id={"narrow": 1 - n}, device_id_type=MESH)

    @pl.when(is_inner)
    def _():
        pl.semaphore_signal(barrier, inc=1, device_id={"groups": 1 - g}, device_id_type=MESH)

    @pl.when(w > 0)
    def _():
        pl.semaphore_signal(barrier, inc=1, device_id={"wide": w - 1}, device_id_type=MESH)

    @pl.when(w < n_wide - 1)
    def _():
        pl.semaphore_signal(barrier, inc=1, device_id={"wide": w + 1}, device_id_type=MESH)

    own_copy = pltpu.make_async_copy(
        amp, held.at[:, :, pl.ds(pl.multiple_of(w * piece, 128), piece)], own_sem
    )
    own_copy.start()
    tile_copy = pltpu.make_async_copy(tiles, own_tiles, tile_sem)
    tile_copy.start()
    sums[slots] = jnp.zeros(sums.shape[1:], jnp.float32)

    pl.semaphore_wait(barrier, jnp.where(is_end, 3, 5))

    def some(c):
        return pl.ds(pl.multiple_of(c * step, step), step)

    def part(origin, c):
        return held.at[:, some(c), pl.ds(pl.multiple_of(origin * piece, 128), piece)]

    def remote(source, target, send, recv, device):
        return pltpu.make_async_remote_copy(
            src_ref=source, dst_ref=target, send_sem=send, recv_sem=recv,
            device_id=device, device_id_type=MESH,
        )

    def to_left(origin, c, source=None):
        return remote(
            part(origin, c) if source is None else source, part(origin, c),
            left_sem.at[origin, c], come_sem.at[origin, c], {"wide": w - 1},
        )

    def to_right(origin, c, source=None):
        return remote(
            part(origin, c) if source is None else source, part(origin, c),
            right_sem.at[origin, c], come_sem.at[origin, c], {"wide": w + 1},
        )

    def left_takes(c):
        return (w > 1) | ((w == 1) & (c < HOME))

    def right_takes(c):
        return (w < n_wide - 2) | ((w == n_wide - 2) & (c < HOME))

    def send_own(c):
        @pl.when(left_takes(c))
        def _():
            to_left(w, c, amp.at[:, some(c), :]).start()

        @pl.when(right_takes(c))
        def _():
            to_right(w, c, amp.at[:, some(c), :]).start()

    def pass_on(distance, c):
        wanted = (c < HOME) | (is_inner & (c < CHUNKS))

        @pl.when(wanted & (w + distance < n_wide))
        def _():
            to_left(w + distance, c).wait_recv()

            @pl.when(left_takes(c))
            def _():
                to_left(w + distance, c).start()

        @pl.when(wanted & (w - distance >= 0))
        def _():
            to_right(w - distance, c).wait_recv()

            @pl.when(right_takes(c))
            def _():
                to_right(w - distance, c).start()

    def part_copy(p):
        here = pl.ds(g * (slots // 2) + p * part_slots, part_slots)
        return remote(
            tiles.at[here], end_tiles.at[here], part_send.at[p], part_recv.at[p], {"wide": mate}
        )

    def across_copy(p):
        here = pl.ds(g * (slots // 2) + p * part_slots, part_slots)
        return remote(
            end_tiles.at[here], end_tiles.at[here],
            across_send.at[p], across_recv.at[p], {"groups": 1 - g},
        )

    list_copy = remote(list_source, list_landed, list_send, list_recv, {"wide": mate})

    def first_copy(u):
        return remote(
            first_out.at[lax.rem(u, 2)], first_in.at[u],
            first_send.at[u], first_recv.at[u], {"sub": 1 - s},
        )

    def second_copy(u):
        return remote(
            second_out.at[lax.rem(u, 2)], second_in.at[u],
            second_send.at[u], second_recv.at[u], {"narrow": 1 - n},
        )

    def out_copy(u, c):
        return pltpu.make_async_copy(second_in.at[u], out.at[some(c), :], out_sem.at[c])

    def back_copy(u, c):
        return remote(
            second_in.at[u], out.at[some(c), :], back_send.at[c], back_recv.at[c], {"wide": mate}
        )

    def chunk_of(u):
        return jnp.where(u < HOME, u, lax.div(u, 2) + HOME // 2)

    def active(u):
        return (u >= 0) & ((u < HOME) | (is_inner & (u < UNITS)))

    def for_mate(u):
        return (u >= HOME) & (lax.rem(u, 2) == 0)

    def compute(u, tile_ref, listed):
        def multiply(t, so_far):
            chosen = jnp.concatenate(
                [
                    mine[listed[1, t] * per_block + strip].reshape(quarters * step, 128)
                    for strip in range(per_block)
                ],
                axis=1,
            )
            product = jnp.dot(
                chosen, tile_ref[listed[0, t]], preferred_element_type=jnp.float32
            )
            so_far = so_far * listed[2, t].astype(jnp.float32) + product
            sums[t] = so_far.reshape(quarters, step, block)
            return so_far

        lax.fori_loop(0, slots, multiply, jnp.zeros((quarters * step, block), jnp.float32))
        slot, side = lax.rem(u, 3), lax.rem(u, 2)
        for b in range(CB_DEV):
            columns = pl.ds(b * block, block)
            column_sum = sums[listed[3, b]]
            first_out[side, :, :, columns] = column_sum[:2]
            total[slot, :, :, columns] = column_sum[2:]
        first_copy(u).start()

    send_own(0)

    @pl.when(is_end)
    def _():
        list_copy.start()
        part_copy(0).start()

    for c in range(1, LEAD):
        send_own(c)
    own_copy.wait()
    tile_copy.wait()
    for c in range(n_wide - 2):
        for distance in range(1, n_wide - 1 - c):
            pass_on(distance, jnp.int32(c))

    def turn(u, nothing):
        c = chunk_of(u)
        opens = (u < HOME) | (lax.rem(u, 2) == 0)

        @pl.when(opens & (c + LEAD < CHUNKS))
        def _():
            send_own(c + LEAD)

        @pl.when(is_end & (u + 1 < TILE_PARTS))
        def _():
            part_copy(u + 1).start()

        @pl.when(is_inner & (u >= HOME - TILE_PARTS) & (u < HOME))
        def _():
            part_copy(u - HOME + TILE_PARTS).wait_recv()
            across_copy(u - HOME + TILE_PARTS).start()

        @pl.when(active(u) & opens)
        def _():
            for distance in range(1, n_wide):
                pass_on(distance, c + n_wide - 1 - distance)

            for half in range(2):
                for place, quarter in ((half, 2 * half + 1 - s), (2 + half, 2 * half + s)):
                    for strip in range(strips):
                        mine[strip, place] = held[quarter, some(c), pl.ds(strip * 128, 128)]

        @pl.when(is_inner & (u == HOME))
        def _():
            list_copy.wait_recv()
            to_list = pltpu.make_async_copy(list_landed, end_list, list_sem)
            to_list.start()
            to_list.wait()
            for p in range(TILE_PARTS):
                across_copy(p).wait_recv()

        @pl.when(active(u) & jnp.logical_not(for_mate(u)))
        def _():
            compute(u, own_tiles, own_list)

        @pl.when(active(u) & for_mate(u))
        def _():
            compute(u, end_tiles, end_list)

        e = u - 1

        @pl.when(active(e))
        def _():
            slot = lax.rem(e, 3)
            first_copy(e).wait()
            second_out[lax.rem(e, 2)] = total[slot, 1 - n] + first_in[e, 1 - n]
            second_copy(e).start()
            total[slot, n] = total[slot, n] + first_in[e, n]

        f = u - 2

        @pl.when(active(f))
        def _():
            second_copy(f).wait()
            second_in[f] = second_in[f] + total[lax.rem(f, 3), n]

            @pl.when(for_mate(f))
            def _():
                back_copy(f, chunk_of(f)).start()

            @pl.when(jnp.logical_not(for_mate(f)))
            def _():
                out_copy(f, chunk_of(f)).start()

        return nothing

    lax.fori_loop(0, UNITS + 2, turn, 0)

    def finish(c, nothing):
        for origin in range(n_wide):
            @pl.when(left_takes(c) & (origin >= w))
            def _():
                to_left(origin, c).wait_send()

            @pl.when(right_takes(c) & (origin <= w))
            def _():
                to_right(origin, c).wait_send()

        @pl.when(is_inner | (c < HOME))
        def _():
            out_copy(0, c).wait()

        @pl.when(is_inner & (c >= HOME))
        def _():
            back_copy(0, c).wait_send()

        @pl.when(is_end & (c >= HOME))
        def _():
            back_copy(0, c).wait_recv()

        return nothing

    lax.fori_loop(0, CHUNKS, finish, 0)

    @pl.when(is_end)
    def _():
        list_copy.wait_send()
        for p in range(TILE_PARTS):
            part_copy(p).wait_send()

    @pl.when(is_inner)
    def _():
        for p in range(TILE_PARTS):
            across_copy(p).wait_send()


def fused_shards(n_wide, amplitudes, integrals, tile_list, tile_counts):
    _, slab_rows, piece = amplitudes.shape
    slots, block = integrals.shape[2], integrals.shape[3]
    quarter_rows = slab_rows // 4
    step = quarter_rows // CHUNKS
    width = CB_DEV * block
    listed = tile_order(tile_list[0, 0], tile_counts[0, 0])
    anywhere = pl.BlockSpec(memory_space=pl.ANY)
    dma = pltpu.SemaphoreType.DMA
    result, _ = pl.pallas_call(
        functools.partial(ladder_kernel, n_wide),
        out_shape=(
            jax.ShapeDtypeStruct((quarter_rows, width), jnp.float32),
            jax.ShapeDtypeStruct(listed.shape, jnp.int32),
        ),
        in_specs=[pl.BlockSpec(memory_space=pltpu.SMEM)] + [anywhere] * 3,
        out_specs=(anywhere, anywhere),
        scratch_shapes=[
            pltpu.VMEM((4, quarter_rows, n_wide * piece), jnp.bfloat16),
            pltpu.VMEM((n_wide * piece // 128, 4, step, 128), jnp.bfloat16),
            pltpu.VMEM((slots, block, block), jnp.bfloat16),
            pltpu.VMEM((slots, block, block), jnp.bfloat16),
            pltpu.SMEM(listed.shape, jnp.int32),
            pltpu.VMEM((slots + 1, 4, step, block), jnp.float32),
            pltpu.VMEM((2, 2, step, width), jnp.float32),
            pltpu.VMEM((UNITS, 2, step, width), jnp.float32),
            pltpu.VMEM((3, 2, step, width), jnp.float32),
            pltpu.VMEM((2, step, width), jnp.float32),
            pltpu.VMEM((UNITS, step, width), jnp.float32),
            dma, dma, dma,
            dma((n_wide, CHUNKS)), dma((n_wide, CHUNKS)), dma((n_wide, CHUNKS)),
            dma((UNITS,)), dma((UNITS,)), dma((UNITS,)), dma((UNITS,)), dma((CHUNKS,)),
            dma((TILE_PARTS,)), dma((TILE_PARTS,)), dma((TILE_PARTS,)), dma((TILE_PARTS,)),
            dma, dma, dma((CHUNKS,)), dma((CHUNKS,)),
        ],
        compiler_params=pltpu.CompilerParams(
            collective_id=0, has_side_effects=True, vmem_limit_bytes=63 * 1024 * 1024
        ),
    )(listed, amplitudes.reshape(4, quarter_rows, piece), integrals[0, 0], listed)
    return result


def shards(sizes, amplitudes, integrals, tile_list, tile_counts):
    fits = (
        sizes["narrow"] == 2
        and sizes["sub"] == 2
        and sizes["wide"] == 4
        and sizes["groups"] == 2
        and amplitudes.shape[2] % 128 == 0
    )
    if fits:
        return fused_shards(sizes["wide"], amplitudes, integrals, tile_list, tile_counts)
    return gathered_shards(amplitudes, integrals, tile_list, tile_counts)


def solution(mesh):
    placed = (
        P(("narrow", "sub"), "groups", "wide"),
        P(("narrow", "sub"), "wide", None, None, None),
        P(("narrow", "sub"), "wide", None, None),
        P(("narrow", "sub"), "wide"),
    )
    return jax.shard_map(
        functools.partial(shards, dict(mesh.shape)),
        mesh=mesh,
        in_specs=placed,
        out_specs=P(("groups", "narrow", "sub"), "wide"),
        check_vma=False,
    )
```

```python
import functools

import jax
import jax.numpy as jnp
from jax import lax
from jax.experimental import pallas as pl
from jax.experimental.pallas import tpu as pltpu
from jax.sharding import PartitionSpec as P

CB_DEV = 15
CHUNKS = 8
HOME = 6
LEAD = 5
UNITS = HOME + 2 * (CHUNKS - HOME)
TILE_PARTS = 4
MESH = pl.DeviceIdType.MESH


def group_width(slot_count):
    best = 1
    for candidate in range(1, 9):
        if slot_count % candidate == 0:
            best = candidate
    return best


def gathered_shards(amplitudes, integrals, tile_list, tile_counts):
    gathered = lax.all_gather(amplitudes[0], "wide", axis=1, tiled=True)
    tile_block = integrals[0, 0]
    listed = tile_list[0, 0]
    live_count = tile_counts[0, 0]
    slab_rows = gathered.shape[0]
    block_size = tile_block.shape[1]
    slot_count = tile_block.shape[0]
    row_blocks = gathered.shape[1] // block_size
    blocks = gathered.reshape(slab_rows, row_blocks, block_size)
    width = group_width(slot_count)
    group_total = (live_count + width - 1) // width

    def add_group(group_index, total):
        first = group_index * width
        these = lax.dynamic_slice_in_dim(listed, first, width, 0)
        tiles_here = lax.dynamic_slice_in_dim(tile_block, first, width, 0)
        chosen = jnp.take(blocks, these[:, 0], axis=1)
        products = jnp.einsum(
            "stp,tpq->tsq", chosen, tiles_here, preferred_element_type=jnp.float32
        )
        live = (first + jnp.arange(width) < live_count).astype(jnp.float32)
        for member in range(width):
            column_start = these[member, 1] * block_size
            current = lax.dynamic_slice_in_dim(total, column_start, block_size, 1)
            updated = current + products[member] * live[member]
            total = lax.dynamic_update_slice_in_dim(total, updated, column_start, 1)
        return total

    empty = jnp.zeros((slab_rows, CB_DEV * block_size), jnp.float32)
    partial_value = lax.fori_loop(0, group_total, add_group, empty)
    result = lax.psum_scatter(partial_value, ("narrow", "sub"), scatter_dimension=0, tiled=True)
    return result


def tile_order(listed, live_count):
    count = listed.shape[0]
    place = jnp.arange(count, dtype=jnp.int32)
    column = jnp.where(place < live_count, listed[:, 1], CB_DEV)
    key = column * count + place
    rank = jnp.sum((key[None, :] < key[:, None]).astype(jnp.int32), axis=1)
    at = (rank[None, :] == place[:, None]).astype(jnp.int32)
    order = jnp.sum(at * place[None, :], axis=1)
    rows = jnp.sum(at * listed[None, :, 0], axis=1)
    first = jnp.sum((column[None, :] < column[:, None]).astype(jnp.int32), axis=1)
    keep = jnp.sum(at * (first != rank).astype(jnp.int32)[None, :], axis=1)
    columns = jnp.arange(CB_DEV, dtype=jnp.int32)
    here = jnp.sum((column[None, :] == columns[:, None]).astype(jnp.int32), axis=1)
    upto = jnp.sum((column[None, :] <= columns[:, None]).astype(jnp.int32), axis=1)
    last = jnp.where(here > 0, upto - 1, count)
    lines = [jnp.pad(line, (0, 128 - line.shape[0])) for line in (order, rows, keep, last)]
    return jnp.pad(jnp.stack(lines), ((0, 4), (0, 0)))


def ladder_kernel(
    n_wide,
    own_list, amp, tiles, list_source, out, list_landed,
    held, mine, own_tiles, end_tiles, end_list, sums,
    first_out, first_in, total, second_out, second_in,
    own_sem, tile_sem, list_sem, left_sem, right_sem, come_sem,
    first_send, first_recv, second_send, second_recv, out_sem,
    part_send, part_recv, across_send, across_recv,
    list_send, list_recv, back_send, back_recv,
):
    g = lax.axis_index("groups")
    w = lax.axis_index("wide")
    n = lax.axis_index("narrow")
    s = lax.axis_index("sub")
    quarters, quarter_rows, piece = amp.shape
    step = quarter_rows // CHUNKS
    slots, block, _ = tiles.shape
    strips = n_wide * piece // 128
    per_block = block // 128
    is_end = (w == 0) | (w == n_wide - 1)
    is_inner = (w > 0) & (w < n_wide - 1)
    mate = w + 1 - 2 * lax.rem(w, 2)
    part_slots = slots // 2 // TILE_PARTS

    barrier = pltpu.get_barrier_semaphore()
    pl.semaphore_signal(barrier, inc=1, device_id={"sub": 1 - s}, device_id_type=MESH)
    pl.semaphore_signal(barrier, inc=1, device_id={"narrow": 1 - n}, device_id_type=MESH)

    @pl.when(is_inner)
    def _():
        pl.semaphore_signal(barrier, inc=1, device_id={"groups": 1 - g}, device_id_type=MESH)

    @pl.when(w > 0)
    def _():
        pl.semaphore_signal(barrier, inc=1, device_id={"wide": w - 1}, device_id_type=MESH)

    @pl.when(w < n_wide - 1)
    def _():
        pl.semaphore_signal(barrier, inc=1, device_id={"wide": w + 1}, device_id_type=MESH)

    own_copy = pltpu.make_async_copy(
        amp, held.at[:, :, pl.ds(pl.multiple_of(w * piece, 128), piece)], own_sem
    )
    own_copy.start()
    tile_copy = pltpu.make_async_copy(tiles, own_tiles, tile_sem)
    tile_copy.start()
    sums[slots] = jnp.zeros(sums.shape[1:], jnp.float32)

    pl.semaphore_wait(barrier, jnp.where(is_end, 3, 5))

    def some(c):
        return pl.ds(pl.multiple_of(c * step, step), step)

    def part(origin, c):
        return held.at[:, some(c), pl.ds(pl.multiple_of(origin * piece, 128), piece)]

    def remote(source, target, send, recv, device):
        return pltpu.make_async_remote_copy(
            src_ref=source, dst_ref=target, send_sem=send, recv_sem=recv,
            device_id=device, device_id_type=MESH,
        )

    def to_left(origin, c, source=None):
        return remote(
            part(origin, c) if source is None else source, part(origin, c),
            left_sem.at[origin, c], come_sem.at[origin, c], {"wide": w - 1},
        )

    def to_right(origin, c, source=None):
        return remote(
            part(origin, c) if source is None else source, part(origin, c),
            right_sem.at[origin, c], come_sem.at[origin, c], {"wide": w + 1},
        )

    def left_takes(c):
        return (w > 1) | ((w == 1) & (c < HOME))

    def right_takes(c):
        return (w < n_wide - 2) | ((w == n_wide - 2) & (c < HOME))

    def send_own(c):
        @pl.when(left_takes(c))
        def _():
            to_left(w, c, amp.at[:, some(c), :]).start()

        @pl.when(right_takes(c))
        def _():
            to_right(w, c, amp.at[:, some(c), :]).start()

    def pass_on(distance, c):
        wanted = (c < HOME) | (is_inner & (c < CHUNKS))

        @pl.when(wanted & (w + distance < n_wide))
        def _():
            to_left(w + distance, c).wait_recv()

            @pl.when(left_takes(c))
            def _():
                to_left(w + distance, c).start()

        @pl.when(wanted & (w - distance >= 0))
        def _():
            to_right(w - distance, c).wait_recv()

            @pl.when(right_takes(c))
            def _():
                to_right(w - distance, c).start()

    def part_copy(p):
        here = pl.ds(g * (slots // 2) + p * part_slots, part_slots)
        return remote(
            tiles.at[here], end_tiles.at[here], part_send.at[p], part_recv.at[p], {"wide": mate}
        )

    def across_copy(p):
        here = pl.ds(g * (slots // 2) + p * part_slots, part_slots)
        return remote(
            end_tiles.at[here], end_tiles.at[here],
            across_send.at[p], across_recv.at[p], {"groups": 1 - g},
        )

    list_copy = remote(list_source, list_landed, list_send, list_recv, {"wide": mate})

    def first_copy(u):
        return remote(
            first_out.at[lax.rem(u, 2)], first_in.at[u],
            first_send.at[u], first_recv.at[u], {"sub": 1 - s},
        )

    def second_copy(u):
        return remote(
            second_out.at[lax.rem(u, 2)], second_in.at[u],
            second_send.at[u], second_recv.at[u], {"narrow": 1 - n},
        )

    def out_copy(u, c):
        return pltpu.make_async_copy(second_in.at[u], out.at[some(c), :], out_sem.at[c])

    def back_copy(u, c):
        return remote(
            second_in.at[u], out.at[some(c), :], back_send.at[c], back_recv.at[c], {"wide": mate}
        )

    def chunk_of(u):
        return jnp.where(u < HOME, u, lax.div(u, 2) + HOME // 2)

    def active(u):
        return (u >= 0) & ((u < HOME) | (is_inner & (u < UNITS)))

    def for_mate(u):
        return (u >= HOME) & (lax.rem(u, 2) == 0)

    def compute(u, tile_ref, listed):
        def multiply(t, so_far):
            chosen = jnp.concatenate(
                [
                    mine[listed[1, t] * per_block + strip].reshape(quarters * step, 128)
                    for strip in range(per_block)
                ],
                axis=1,
            )
            product = jnp.dot(
                chosen, tile_ref[listed[0, t]], preferred_element_type=jnp.float32
            )
            so_far = so_far * listed[2, t].astype(jnp.float32) + product
            sums[t] = so_far.reshape(quarters, step, block)
            return so_far

        lax.fori_loop(0, slots, multiply, jnp.zeros((quarters * step, block), jnp.float32))
        slot, side = lax.rem(u, 3), lax.rem(u, 2)
        for b in range(CB_DEV):
            columns = pl.ds(b * block, block)
            column_sum = sums[listed[3, b]]
            first_out[side, :, :, columns] = column_sum[:2]
            total[slot, :, :, columns] = column_sum[2:]
        first_copy(u).start()

    send_own(0)

    @pl.when(is_end)
    def _():
        list_copy.start()
        part_copy(0).start()

    for c in range(1, LEAD):
        send_own(c)
    own_copy.wait()
    tile_copy.wait()
    for c in range(n_wide - 2):
        for distance in range(1, n_wide - 1 - c):
            pass_on(distance, jnp.int32(c))

    def turn(u, nothing):
        c = chunk_of(u)
        opens = (u < HOME) | (lax.rem(u, 2) == 0)

        @pl.when(opens & (c + LEAD < CHUNKS))
        def _():
            send_own(c + LEAD)

        @pl.when(is_end & (u + 1 < TILE_PARTS))
        def _():
            part_copy(u + 1).start()

        @pl.when(is_inner & (u >= HOME - TILE_PARTS) & (u < HOME))
        def _():
            part_copy(u - HOME + TILE_PARTS).wait_recv()
            across_copy(u - HOME + TILE_PARTS).start()

        @pl.when(active(u) & opens)
        def _():
            for distance in range(1, n_wide):
                pass_on(distance, c + n_wide - 1 - distance)

            for half in range(2):
                for place, quarter in ((half, 2 * half + 1 - s), (2 + half, 2 * half + s)):
                    for strip in range(strips):
                        mine[strip, place] = held[quarter, some(c), pl.ds(strip * 128, 128)]

        @pl.when(is_inner & (u == HOME))
        def _():
            list_copy.wait_recv()
            to_list = pltpu.make_async_copy(list_landed, end_list, list_sem)
            to_list.start()
            to_list.wait()
            for p in range(TILE_PARTS):
                across_copy(p).wait_recv()

        @pl.when(active(u) & jnp.logical_not(for_mate(u)))
        def _():
            compute(u, own_tiles, own_list)

        @pl.when(active(u) & for_mate(u))
        def _():
            compute(u, end_tiles, end_list)

        e = u - 1

        @pl.when(active(e))
        def _():
            slot = lax.rem(e, 3)
            first_copy(e).wait()
            second_out[lax.rem(e, 2)] = total[slot, 1 - n] + first_in[e, 1 - n]
            second_copy(e).start()
            total[slot, n] = total[slot, n] + first_in[e, n]

        f = u - 2

        @pl.when(active(f))
        def _():
            second_copy(f).wait()
            second_in[f] = second_in[f] + total[lax.rem(f, 3), n]

            @pl.when(for_mate(f))
            def _():
                back_copy(f, chunk_of(f)).start()

            @pl.when(jnp.logical_not(for_mate(f)))
            def _():
                out_copy(f, chunk_of(f)).start()

        return nothing

    lax.fori_loop(0, UNITS + 2, turn, 0)

    def finish(c, nothing):
        for origin in range(n_wide):
            @pl.when(left_takes(c) & (origin >= w))
            def _():
                to_left(origin, c).wait_send()

            @pl.when(right_takes(c) & (origin <= w))
            def _():
                to_right(origin, c).wait_send()

        @pl.when(is_inner | (c < HOME))
        def _():
            out_copy(0, c).wait()

        @pl.when(is_inner & (c >= HOME))
        def _():
            back_copy(0, c).wait_send()

        @pl.when(is_end & (c >= HOME))
        def _():
            back_copy(0, c).wait_recv()

        return nothing

    lax.fori_loop(0, CHUNKS, finish, 0)

    @pl.when(is_end)
    def _():
        list_copy.wait_send()
        for p in range(TILE_PARTS):
            part_copy(p).wait_send()

    @pl.when(is_inner)
    def _():
        for p in range(TILE_PARTS):
            across_copy(p).wait_send()


def fused_shards(n_wide, amplitudes, integrals, tile_list, tile_counts):
    _, slab_rows, piece = amplitudes.shape
    slots, block = integrals.shape[2], integrals.shape[3]
    quarter_rows = slab_rows // 4
    step = quarter_rows // CHUNKS
    width = CB_DEV * block
    listed = tile_order(tile_list[0, 0], tile_counts[0, 0])
    anywhere = pl.BlockSpec(memory_space=pl.ANY)
    dma = pltpu.SemaphoreType.DMA
    result, _ = pl.pallas_call(
        functools.partial(ladder_kernel, n_wide),
        out_shape=(
            jax.ShapeDtypeStruct((quarter_rows, width), jnp.float32),
            jax.ShapeDtypeStruct(listed.shape, jnp.int32),
        ),
        in_specs=[pl.BlockSpec(memory_space=pltpu.SMEM)] + [anywhere] * 3,
        out_specs=(anywhere, anywhere),
        scratch_shapes=[
            pltpu.VMEM((4, quarter_rows, n_wide * piece), jnp.bfloat16),
            pltpu.VMEM((n_wide * piece // 128, 4, step, 128), jnp.bfloat16),
            pltpu.VMEM((slots, block, block), jnp.bfloat16),
            pltpu.VMEM((slots, block, block), jnp.bfloat16),
            pltpu.SMEM(listed.shape, jnp.int32),
            pltpu.VMEM((slots + 1, 4, step, block), jnp.float32),
            pltpu.VMEM((2, 2, step, width), jnp.float32),
            pltpu.VMEM((UNITS, 2, step, width), jnp.float32),
            pltpu.VMEM((3, 2, step, width), jnp.float32),
            pltpu.VMEM((2, step, width), jnp.float32),
            pltpu.VMEM((UNITS, step, width), jnp.float32),
            dma, dma, dma,
            dma((n_wide, CHUNKS)), dma((n_wide, CHUNKS)), dma((n_wide, CHUNKS)),
            dma((UNITS,)), dma((UNITS,)), dma((UNITS,)), dma((UNITS,)), dma((CHUNKS,)),
            dma((TILE_PARTS,)), dma((TILE_PARTS,)), dma((TILE_PARTS,)), dma((TILE_PARTS,)),
            dma, dma, dma((CHUNKS,)), dma((CHUNKS,)),
        ],
        compiler_params=pltpu.CompilerParams(
            collective_id=0, has_side_effects=True, vmem_limit_bytes=63 * 1024 * 1024
        ),
    )(listed, amplitudes.reshape(4, quarter_rows, piece), integrals[0, 0], listed)
    return result


def shards(sizes, amplitudes, integrals, tile_list, tile_counts):
    fits = (
        sizes["narrow"] == 2
        and sizes["sub"] == 2
        and sizes["wide"] == 4
        and sizes["groups"] == 2
        and amplitudes.shape[2] % 128 == 0
    )
    if fits:
        return fused_shards(sizes["wide"], amplitudes, integrals, tile_list, tile_counts)
    return gathered_shards(amplitudes, integrals, tile_list, tile_counts)


def solution(mesh):
    placed = (
        P(("narrow", "sub"), "groups", "wide"),
        P(("narrow", "sub"), "wide", None, None, None),
        P(("narrow", "sub"), "wide", None, None),
        P(("narrow", "sub"), "wide"),
    )
    return jax.shard_map(
        functools.partial(shards, dict(mesh.shape)),
        mesh=mesh,
        in_specs=placed,
        out_specs=P(("groups", "narrow", "sub"), "wide"),
        check_vma=False,
    )
```
